32 devices in a mesh: dp: 8 (over y, x, core), ctx: 4 (over z).
Axes of the slice: x: 2, y: 2, z: 4, core: 2. Of those that a mesh axis runs over, the one named last changes fastest.
Arguments:
- output_gradient: float32 [8, 8, 32768], P('dp', None, 'ctx'), may hold values from -6 to 6
- input_spectrum: float32 [8, 8, 2, 32768], P('dp', None, None, 'ctx'), may hold values from -0.0390625 to 0.0390625
- filter_spectrum: float32 [8, 2, 32768], P(None, None, 'ctx'), may hold values from -12 to 12
Outputs:
- input_gradient: float32 [8, 8, 32768], P('dp', None, 'ctx')
- filter_gradient: float32 [8, 2, 32768], P(None, None, ('ctx', 'dp'))
The draws below stay inside these ranges and needn't reach their ends.
All inputs are finite; a program needn't handle non-finite values.
Results may differ from the reference program's by a relative error of at most 0.0001.
Values sent between devices are 32-bit elements; how exact they have to be, the bound alone decides.
A program may use at most 128 MiB of HBM per device.

```python
import jax
import jax.numpy as jnp
from jax import lax

CHANS = 8
TOK_DEV = 8192
LEN = 32768
BATCH = 8
SECTIONS = 2
N_CTX = 4


def strengthened(array, key, source, target, blocks, factor):
    owner, partner = [(jnp.arange(array.shape[position]) // (array.shape[position] // blocks)).reshape([-1 if axis == position else 1 for axis in range(array.ndim)]) for position in (source, target)]
    chosen = jax.random.permutation(key, blocks)[partner]
    strong = (owner == chosen) | (owner == (partner + blocks // 2) % blocks)
    return jnp.where(strong, factor * array, array)


def level_of(key, extent, cuts, low, top_value):
    def one(dim, shards_of):
        draws = jax.random.uniform(jax.random.fold_in(jax.random.fold_in(key, 6), dim), (shards_of,), jnp.float32, low / len(cuts), top_value / len(cuts))
        return jnp.repeat(jnp.exp(draws), extent[dim] // shards_of).reshape((-1,) + (1,) * (len(extent) - dim - 1))

    loudness = one(*cuts[0])
    for cut in cuts[1:]:
        loudness = loudness * one(*cut)
    return loudness


def bell_draw(key, shape, scale, most, cuts=(), held_as=jnp.bfloat16):
    entries = jax.random.normal(key, shape, jnp.float32) * scale
    if len(cuts) > 0:
        entries = level_of(key, shape, cuts, -0.22, 0.18) * entries
    return jnp.clip(entries, min=-most, max=most).astype(held_as)


def gaussian_with(rng, dims, width, limit, split, heavy, held_as=jnp.bfloat16):
    values = width * jax.random.normal(rng, dims, jnp.float32)
    if split:
        values = values * level_of(rng, dims, split, -0.22, 0.18)
    return jnp.clip(strengthened(values, jax.random.fold_in(rng, 3), *heavy), -limit, limit).astype(held_as)


def setup_inputs(seed: int = 0) -> dict:
    seeds = jax.random.split(jax.random.key(seed), 4)
    return {
        "output_gradient": bell_draw(seeds[0], (BATCH, CHANS, LEN), 1.0, 6.0, ((0, 8), (2, 4)), jnp.float32),
        "input_spectrum": gaussian_with(seeds[1], (BATCH, CHANS, 2, LEN), ((LEN * BATCH) ** -0.5), 0.0390625, ((0, 8), (3, 4)), (0, 3, 8, 2.0), jnp.float32),
        "filter_spectrum": bell_draw(seeds[2], (CHANS, 2, LEN), 2.0, 12.0, ((2, 4),), jnp.float32),
    }


def reverse_digits(index):
    result = jnp.zeros_like(index)
    for level in range(SECTIONS):
        result = result | (((index >> level) & 1) << (SECTIONS - 1 - level))
    return result


def frequency_order():
    series = jnp.arange(LEN, dtype=jnp.int32)
    blocks = series // TOK_DEV
    within = series % TOK_DEV
    return (N_CTX * within + reverse_digits(blocks)).astype(jnp.int32)


def reference(output_gradient, input_spectrum, filter_spectrum):
    frequency = frequency_order()
    filter_complex = filter_spectrum[:, 0] + 1j * filter_spectrum[:, 1]
    positions = jnp.arange(LEN, dtype=jnp.int32)
    twist = jnp.exp((-0.5j * jnp.pi / LEN) * positions)
    untwist = jnp.exp((0.5j * jnp.pi / LEN) * positions)

    def per_sequence(carry, inputs):
        samples, saved = inputs
        spectrum = jnp.fft.fft(samples * twist, axis=-1)[:, frequency]
        product = spectrum * jnp.conj(filter_complex)
        whole = jnp.zeros((CHANS, LEN), spectrum.dtype).at[:, frequency].set(product)
        gradient = jnp.real(jnp.fft.ifft(whole, axis=-1) * untwist)
        saved_complex = saved[:, 0] + 1j * saved[:, 1]
        term = spectrum * jnp.conj(saved_complex)
        totals = (carry[0] + jnp.real(term).astype(jnp.float32), carry[1] + jnp.imag(term).astype(jnp.float32))
        return totals, gradient.astype(jnp.float32)

    start = jnp.zeros((CHANS, LEN), jnp.float32)
    totals, input_gradient = lax.scan(per_sequence, (start, start), (output_gradient, input_spectrum))
    return input_gradient, jnp.stack([totals[0], totals[1]], axis=1)
```

```python
import functools
import math

import jax
import jax.numpy as jnp
import ml_dtypes
import numpy as np
from jax import lax
from jax.experimental import pallas as pl
from jax.experimental.pallas import tpu as pltpu
from jax.sharding import PartitionSpec as P

MESH = pl.DeviceIdType.MESH
LANES = 128


def low_bit(value):
    return value & -value


def reverse(index, sections):
    result = 0 * index
    for level in range(sections):
        result = result | ((index >> level) & 1) << (sections - 1 - level)
    return result


def halves(table):
    table = np.asarray(table, np.float32)
    high = table.astype(ml_dtypes.bfloat16)
    low = (table - high.astype(np.float32)).astype(ml_dtypes.bfloat16)
    return np.stack([high, low])


def make_tables(n_ctx, tokens):
    rows = tokens // LANES
    length = n_ctx * tokens
    sections = n_ctx.bit_length() - 1
    turn = 2.0 * math.pi
    ta, tb = np.arange(rows), np.arange(LANES)
    small = turn / rows * (ta[:, None] * ta[None, :] % rows)
    wide = turn / rows * (ta[:, None] * tb[None, :] % rows)
    second = np.block([[np.cos(wide), np.sin(wide)], [-np.sin(wide), np.cos(wide)]])
    third = np.block([[np.cos(small), -np.sin(small)], [np.sin(small), np.cos(small)]])
    first_all, last_all, turns_all = [], [], []
    for self_index in range(n_ctx):
        shift = reverse(self_index, sections) + 0.25
        owner = self_index ^ np.arange(n_ctx)
        start = (owner[:, None] * tokens + LANES * ta[None, :]).reshape(-1)
        offset = turn / length * (shift * start % length)
        angle = np.tile(small, (1, n_ctx)) + offset[None, :]
        first_all.append(halves(np.concatenate([np.cos(angle), -np.sin(angle)], axis=0)))
        angle = np.tile(wide, (n_ctx, 1)) + offset[:, None]
        last_all.append(
            halves(np.concatenate([np.cos(angle), -np.sin(angle)], axis=1) / length)
        )
        angle = turn / length * (tb[None, :] * (n_ctx * tb[:, None] + shift) % length)
        turns_all.append(
            np.stack([np.cos(angle), -np.sin(angle), np.cos(angle).T, np.sin(angle).T])
        )
    return (
        np.stack(first_all),
        np.stack(last_all),
        np.stack(turns_all).astype(np.float32),
        halves(second),
        halves(third),
    )


def split(value):
    high = value.astype(jnp.bfloat16)
    return high, (value - high.astype(jnp.float32)).astype(jnp.bfloat16)


def product(table, value, contract):
    high, low = split(value)
    dims = (((1,), (contract,)), ((), ()))
    dot = functools.partial(
        lax.dot_general, dimension_numbers=dims, preferred_element_type=jnp.float32
    )
    return dot(table[0], high) + (dot(table[0], low) + dot(table[1], high))


def kernel(
    sizes,
    x_ref,
    saved_ref,
    filt_ref,
    first_hbm,
    last_hbm,
    turns_hbm,
    second_ref,
    third_ref,
    out_ref,
    grad_ref,
    first_ref,
    last_ref,
    turns_ref,
    xs,
    zs,
    rs,
    terms,
    others,
    table_sem,
    fwd_send,
    fwd_recv,
    inv_send,
    inv_recv,
    dp_send,
    dp_recv,
):
    n_dp, n_ctx, chans, rows, groups = sizes
    per_group = chans // groups
    share = rows // n_dp
    repeats = LANES // rows
    dp = lax.axis_index("dp")
    ctx = lax.axis_index("ctx")
    bits = [1 << level for level in range(n_ctx.bit_length() - 1)]
    peers = [lax.rem(dp + step, n_dp) for step in range(n_dp)]

    tables = [
        pltpu.make_async_copy(source.at[ctx], target, table_sem.at[number])
        for number, (source, target) in enumerate(
            [(first_hbm, first_ref), (last_hbm, last_ref), (turns_hbm, turns_ref)]
        )
    ]
    for copy in tables:
        copy.start()

    barrier = pltpu.get_barrier_semaphore()
    for bit in bits:
        pl.semaphore_signal(barrier, inc=1, device_id=(dp, ctx ^ bit), device_id_type=MESH)
    for peer in peers[1:]:
        pl.semaphore_signal(barrier, inc=1, device_id=(peer, ctx), device_id_type=MESH)

    for chan in range(chans):
        xs[chan // per_group, 0, chan % per_group] = x_ref[pl.ds(chan, rows, stride=chans), :]
    pl.semaphore_wait(barrier, len(bits) + n_dp - 1)

    def forward(group, slot):
        bit = low_bit(slot)
        return pltpu.make_async_remote_copy(
            src_ref=xs.at[group, slot - bit],
            dst_ref=xs.at[group, slot],
            send_sem=fwd_send.at[group, slot],
            recv_sem=fwd_recv.at[group, slot],
            device_id=(dp, ctx ^ bit),
            device_id_type=MESH,
        )

    def inverse(group, slot):
        return pltpu.make_async_remote_copy(
            src_ref=zs.at[group, slot],
            dst_ref=rs.at[group, slot],
            send_sem=inv_send.at[group, slot],
            recv_sem=inv_recv.at[group, slot],
            device_id=(dp, ctx ^ low_bit(slot)),
            device_id_type=MESH,
        )

    def exchange(group, step):
        return pltpu.make_async_remote_copy(
            src_ref=terms.at[group, peers[step]],
            dst_ref=others.at[group, step],
            send_sem=dp_send.at[group, step],
            recv_sem=dp_recv.at[group, step],
            device_id=(peers[step], ctx),
            device_id_type=MESH,
        )

    def pass_on(group):
        for bit in bits[::-1]:
            for slot in range(2 * bit, n_ctx, 2 * bit):
                if low_bit(slot) == 2 * bit:
                    forward(group, slot).wait_recv()
                forward(group, slot + bit).start()

    def gather(group):
        for slot in range(1, n_ctx, 2):
            forward(group, slot).wait_recv()

    def transform(group):
        pair = range(per_group)
        block = jnp.concatenate(
            [xs[group, :, chan].reshape(n_ctx * rows, LANES) for chan in pair], axis=1
        )
        stage = product(first_ref, block, 0)
        turned = []
        for chan in pair:
            lanes = slice(chan * LANES, (chan + 1) * LANES)
            real = jnp.concatenate([stage[:rows, lanes]] * repeats, axis=0)
            imag = jnp.concatenate([stage[rows:, lanes]] * repeats, axis=0)
            cosine, sine = turns_ref[0], turns_ref[1]
            turned.append(
                jnp.concatenate(
                    [real * cosine - imag * sine, real * sine + imag * cosine], axis=1
                )
            )
        spectrum = product(second_ref, jnp.concatenate(turned, axis=0), 1)
        multiplied = []
        for chan in pair:
            lanes = slice(chan * LANES, (chan + 1) * LANES)
            real, imag = spectrum[:rows, lanes], spectrum[rows:, lanes]
            base = (group * per_group + chan) * 2 * rows
            saved_real = saved_ref[pl.ds(base, rows, stride=2), :]
            saved_imag = saved_ref[pl.ds(base + 1, rows, stride=2), :]
            parts = (real * saved_real + imag * saved_imag, imag * saved_real - real * saved_imag)
            for number, part in enumerate(parts):
                for owner in range(n_dp):
                    where = pl.ds(chan * 2 * share + number, share, stride=2)
                    terms[group, owner, where, :] = part[owner * share : (owner + 1) * share]
            filt_real = filt_ref[pl.ds(base, rows, stride=2), :]
            filt_imag = filt_ref[pl.ds(base + 1, rows, stride=2), :]
            multiplied.append(
                jnp.concatenate(
                    [real * filt_real + imag * filt_imag, imag * filt_real - real * filt_imag],
                    axis=0,
                )
            )
        stage = product(third_ref, jnp.concatenate(multiplied, axis=1), 0)
        turned = []
        for chan in pair:
            lanes = slice(chan * LANES, (chan + 1) * LANES)
            real = jnp.concatenate([stage[:rows, lanes]] * repeats, axis=0)
            imag = jnp.concatenate([stage[rows:, lanes]] * repeats, axis=0)
            cosine, sine = turns_ref[2], turns_ref[3]
            turned.append(
                jnp.concatenate(
                    [real * cosine - imag * sine, real * sine + imag * cosine], axis=1
                )
            )
        result = product(last_ref, jnp.concatenate(turned, axis=0), 1)
        for chan in pair:
            lanes = slice(chan * LANES, (chan + 1) * LANES)
            zs[group, :, chan] = result[:, lanes].reshape(n_ctx, rows, LANES)

    def send_back(group):
        for slot in range(1, n_ctx, 2):
            inverse(group, slot).start()

    def fold(group):
        for bit in bits[:-1]:
            for slot in range(2 * bit, n_ctx, 2 * bit):
                inverse(group, slot + bit).wait_recv()
                zs[group, slot] = zs[group, slot] + rs[group, slot + bit]
                if low_bit(slot) == 2 * bit:
                    inverse(group, slot).start()

    def finish(group):
        for bit in bits:
            inverse(group, bit).wait_recv()
        for chan in range(per_group):
            total = zs[group, 0, chan]
            for bit in bits:
                total = total + rs[group, bit, chan]
            out_ref[pl.ds(group * per_group + chan, rows, stride=chans), :] = total

    for group in range(groups):
        for bit in bits[::-1]:
            forward(group, bit).start()
    pass_on(0)
    for copy in tables:
        copy.wait()
    if groups > 1:
        pass_on(1)
    for group in range(groups):
        gather(group)
        transform(group)
        send_back(group)
        for step in range(1, n_dp):
            exchange(group, step).start()
        if group + 2 < groups:
            pass_on(group + 2)
        if group > 0:
            fold(group - 1)
    fold(groups - 1)
    for group in range(groups):
        finish(group)
        total = terms[group, dp]
        for step in range(1, n_dp):
            exchange(group, step).wait_recv()
            total = total + others[group, step]
        grad_ref[group] = total
    for group in range(groups):
        for slot in range(1, n_ctx):
            forward(group, slot).wait_send()
            inverse(group, slot).wait_send()
        for step in range(1, n_dp):
            exchange(group, step).wait_send()


def per_device(n_dp, n_ctx, output_gradient, input_spectrum, filter_spectrum):
    _, chans, tokens = output_gradient.shape
    rows = tokens // LANES
    groups = chans // 2
    per_group = chans // groups
    share = rows // n_dp
    first, last, turns, second, third = make_tables(n_ctx, tokens)

    def spectral(array):
        array = array.reshape(chans, 2, rows, LANES).transpose(0, 2, 1, 3)
        return array.reshape(chans * rows * 2, LANES)

    samples = output_gradient.reshape(chans, rows, LANES).transpose(1, 0, 2)
    samples = samples.reshape(rows * chans, LANES)
    vmem = pl.BlockSpec(memory_space=pltpu.VMEM)
    anywhere = pl.BlockSpec(memory_space=pl.ANY)
    block = (groups, n_ctx, per_group, rows, LANES)
    spread = (groups, n_dp, per_group * share * 2, LANES)
    dma = pltpu.SemaphoreType.DMA
    gradient, filter_gradient = pl.pallas_call(
        functools.partial(kernel, (n_dp, n_ctx, chans, rows, groups)),
        out_shape=(
            jax.ShapeDtypeStruct((rows * chans, LANES), jnp.float32),
            jax.ShapeDtypeStruct((groups, per_group * share * 2, LANES), jnp.float32),
        ),
        in_specs=[vmem] * 3 + [anywhere] * 3 + [vmem] * 2,
        out_specs=(vmem, vmem),
        scratch_shapes=[
            pltpu.VMEM(first.shape[1:], jnp.bfloat16),
            pltpu.VMEM(last.shape[1:], jnp.bfloat16),
            pltpu.VMEM(turns.shape[1:], jnp.float32),
            pltpu.VMEM(block, jnp.float32),
            pltpu.VMEM(block, jnp.float32),
            pltpu.VMEM(block, jnp.float32),
            pltpu.VMEM(spread, jnp.float32),
            pltpu.VMEM(spread, jnp.float32),
            dma((3,)),
            dma((groups, n_ctx)),
            dma((groups, n_ctx)),
            dma((groups, n_ctx)),
            dma((groups, n_ctx)),
            dma((groups, n_dp)),
            dma((groups, n_dp)),
        ],
        compiler_params=pltpu.CompilerParams(
            collective_id=0, has_side_effects=True, vmem_limit_bytes=40 * 1024 * 1024
        ),
    )(
        samples,
        spectral(input_spectrum[0]),
        spectral(filter_spectrum),
        jnp.asarray(first),
        jnp.asarray(last),
        jnp.asarray(turns),
        jnp.asarray(second),
        jnp.asarray(third),
    )
    gradient = gradient.reshape(rows, chans, LANES).transpose(1, 0, 2)
    filter_gradient = filter_gradient.reshape(chans, share, 2, LANES).transpose(0, 2, 1, 3)
    return (
        gradient.reshape(1, chans, tokens),
        filter_gradient.reshape(chans, 2, share * LANES),
    )


def solution(mesh):
    in_specs = (P("dp", None, "ctx"), P("dp", None, None, "ctx"), P(None, None, "ctx"))
    out_specs = (P("dp", None, "ctx"), P(None, None, ("ctx", "dp")))
    return jax.shard_map(
        functools.partial(per_device, mesh.shape["dp"], mesh.shape["ctx"]),
        mesh=mesh,
        in_specs=in_specs,
        out_specs=out_specs,
        check_vma=False,
    )
```

```python
import functools
import math

import jax
import jax.numpy as jnp
import ml_dtypes
import numpy as np
from jax import lax
from jax.experimental import pallas as pl
from jax.experimental.pallas import tpu as pltpu
from jax.sharding import PartitionSpec as P

MESH = pl.DeviceIdType.MESH
LANES = 128


def low_bit(value):
    return value & -value


def reverse(index, sections):
    result = 0 * index
    for level in range(sections):
        result = result | ((index >> level) & 1) << (sections - 1 - level)
    return result


def halves(table):
    table = np.asarray(table, np.float32)
    high = table.astype(ml_dtypes.bfloat16)
    low = (table - high.astype(np.float32)).astype(ml_dtypes.bfloat16)
    return np.stack([high, low])


def make_tables(n_ctx, tokens):
    rows = tokens // LANES
    length = n_ctx * tokens
    sections = n_ctx.bit_length() - 1
    turn = 2.0 * math.pi
    ta, tb = np.arange(rows), np.arange(LANES)
    small = turn / rows * (ta[:, None] * ta[None, :] % rows)
    wide = turn / rows * (ta[:, None] * tb[None, :] % rows)
    second = np.block([[np.cos(wide), np.sin(wide)], [-np.sin(wide), np.cos(wide)]])
    third = np.block([[np.cos(small), -np.sin(small)], [np.sin(small), np.cos(small)]])
    first_all, last_all, turns_all = [], [], []
    for self_index in range(n_ctx):
        shift = reverse(self_index, sections) + 0.25
        owner = self_index ^ np.arange(n_ctx)
        start = (owner[:, None] * tokens + LANES * ta[None, :]).reshape(-1)
        offset = turn / length * (shift * start % length)
        angle = np.tile(small, (1, n_ctx)) + offset[None, :]
        first_all.append(halves(np.concatenate([np.cos(angle), -np.sin(angle)], axis=0)))
        angle = np.tile(wide, (n_ctx, 1)) + offset[:, None]
        last_all.append(
            halves(np.concatenate([np.cos(angle), -np.sin(angle)], axis=1) / length)
        )
        angle = turn / length * (tb[None, :] * (n_ctx * tb[:, None] + shift) % length)
        turns_all.append(
            np.stack([np.cos(angle), -np.sin(angle), np.cos(angle).T, np.sin(angle).T])
        )
    return (
        np.stack(first_all),
        np.stack(last_all),
        np.stack(turns_all).astype(np.float32),
        halves(second),
        halves(third),
    )


def split(value):
    high = value.astype(jnp.bfloat16)
    return high, (value - high.astype(jnp.float32)).astype(jnp.bfloat16)


def product(table, value, contract):
    high, low = split(value)
    dims = (((1,), (contract,)), ((), ()))
    dot = functools.partial(
        lax.dot_general, dimension_numbers=dims, preferred_element_type=jnp.float32
    )
    return dot(table[0], high) + (dot(table[0], low) + dot(table[1], high))


def kernel(
    sizes,
    x_hbm,
    saved_hbm,
    filt_hbm,
    first_hbm,
    last_hbm,
    turns_hbm,
    second_hbm,
    third_hbm,
    out_ref,
    grad_ref,
    x_ref,
    first_ref,
    turns_ref,
    second_ref,
    saved_ref,
    filt_ref,
    third_ref,
    last_ref,
    xs,
    zs,
    rs,
    terms,
    others,
    table_sem,
    fwd_send,
    fwd_recv,
    inv_send,
    inv_recv,
    dp_send,
    dp_recv,
):
    n_dp, n_ctx, chans, rows, groups = sizes
    per_group = chans // groups
    share = rows // n_dp
    repeats = LANES // rows
    dp = lax.axis_index("dp")
    ctx = lax.axis_index("ctx")
    bits = [1 << level for level in range(n_ctx.bit_length() - 1)]
    peers = [lax.rem(dp + step, n_dp) for step in range(n_dp)]

    tables = [
        pltpu.make_async_copy(source, target, table_sem.at[number])
        for number, (source, target) in enumerate(
            [
                (x_hbm, x_ref),
                (first_hbm.at[ctx], first_ref),
                (turns_hbm.at[ctx], turns_ref),
                (second_hbm, second_ref),
                (saved_hbm, saved_ref),
                (filt_hbm, filt_ref),
                (third_hbm, third_ref),
                (last_hbm.at[ctx], last_ref),
            ]
        )
    ]
    for copy in tables:
        copy.start()

    barrier = pltpu.get_barrier_semaphore()
    for bit in bits:
        pl.semaphore_signal(barrier, inc=1, device_id=(dp, ctx ^ bit), device_id_type=MESH)
    for peer in peers[1:]:
        pl.semaphore_signal(barrier, inc=1, device_id=(peer, ctx), device_id_type=MESH)

    tables[0].wait()
    for chan in range(chans):
        xs[chan // per_group, 0, chan % per_group] = x_ref[pl.ds(chan, rows, stride=chans), :]
    pl.semaphore_wait(barrier, len(bits) + n_dp - 1)

    def forward(group, slot):
        bit = low_bit(slot)
        return pltpu.make_async_remote_copy(
            src_ref=xs.at[group, slot - bit],
            dst_ref=xs.at[group, slot],
            send_sem=fwd_send.at[group, slot],
            recv_sem=fwd_recv.at[group, slot],
            device_id=(dp, ctx ^ bit),
            device_id_type=MESH,
        )

    def inverse(group, slot):
        return pltpu.make_async_remote_copy(
            src_ref=zs.at[group, slot],
            dst_ref=rs.at[group, slot],
            send_sem=inv_send.at[group, slot],
            recv_sem=inv_recv.at[group, slot],
            device_id=(dp, ctx ^ low_bit(slot)),
            device_id_type=MESH,
        )

    def exchange(group, step):
        return pltpu.make_async_remote_copy(
            src_ref=terms.at[group, peers[step]],
            dst_ref=others.at[group, step],
            send_sem=dp_send.at[group, step],
            recv_sem=dp_recv.at[group, step],
            device_id=(peers[step], ctx),
            device_id_type=MESH,
        )

    def pass_on(group):
        for bit in bits[::-1]:
            for slot in range(2 * bit, n_ctx, 2 * bit):
                if low_bit(slot) == 2 * bit:
                    forward(group, slot).wait_recv()
                forward(group, slot + bit).start()

    def gather(group):
        for slot in range(1, n_ctx, 2):
            forward(group, slot).wait_recv()

    def transform(group):
        pair = range(per_group)
        block = jnp.concatenate(
            [xs[group, :, chan].reshape(n_ctx * rows, LANES) for chan in pair], axis=1
        )
        stage = product(first_ref, block, 0)
        turned = []
        for chan in pair:
            lanes = slice(chan * LANES, (chan + 1) * LANES)
            real = jnp.concatenate([stage[:rows, lanes]] * repeats, axis=0)
            imag = jnp.concatenate([stage[rows:, lanes]] * repeats, axis=0)
            cosine, sine = turns_ref[0], turns_ref[1]
            turned.append(
                jnp.concatenate(
                    [real * cosine - imag * sine, real * sine + imag * cosine], axis=1
                )
            )
        spectrum = product(second_ref, jnp.concatenate(turned, axis=0), 1)
        multiplied = []
        for chan in pair:
            lanes = slice(chan * LANES, (chan + 1) * LANES)
            real, imag = spectrum[:rows, lanes], spectrum[rows:, lanes]
            base = (group * per_group + chan) * 2 * rows
            saved_real = saved_ref[pl.ds(base, rows, stride=2), :]
            saved_imag = saved_ref[pl.ds(base + 1, rows, stride=2), :]
            parts = (real * saved_real + imag * saved_imag, imag * saved_real - real * saved_imag)
            for number, part in enumerate(parts):
                for owner in range(n_dp):
                    where = pl.ds(chan * 2 * share + number, share, stride=2)
                    terms[group, owner, where, :] = part[owner * share : (owner + 1) * share]
            filt_real = filt_ref[pl.ds(base, rows, stride=2), :]
            filt_imag = filt_ref[pl.ds(base + 1, rows, stride=2), :]
            multiplied.append(
                jnp.concatenate(
                    [real * filt_real + imag * filt_imag, imag * filt_real - real * filt_imag],
                    axis=0,
                )
            )
        stage = product(third_ref, jnp.concatenate(multiplied, axis=1), 0)
        turned = []
        for chan in pair:
            lanes = slice(chan * LANES, (chan + 1) * LANES)
            real = jnp.concatenate([stage[:rows, lanes]] * repeats, axis=0)
            imag = jnp.concatenate([stage[rows:, lanes]] * repeats, axis=0)
            cosine, sine = turns_ref[2], turns_ref[3]
            turned.append(
                jnp.concatenate(
                    [real * cosine - imag * sine, real * sine + imag * cosine], axis=1
                )
            )
        result = product(last_ref, jnp.concatenate(turned, axis=0), 1)
        for chan in pair:
            lanes = slice(chan * LANES, (chan + 1) * LANES)
            zs[group, :, chan] = result[:, lanes].reshape(n_ctx, rows, LANES)

    def send_back(group):
        for slot in range(1, n_ctx, 2):
            inverse(group, slot).start()

    def fold(group):
        for bit in bits[:-1]:
            for slot in range(2 * bit, n_ctx, 2 * bit):
                inverse(group, slot + bit).wait_recv()
                zs[group, slot] = zs[group, slot] + rs[group, slot + bit]
                if low_bit(slot) == 2 * bit:
                    inverse(group, slot).start()

    def finish(group):
        for bit in bits:
            inverse(group, bit).wait_recv()
        for chan in range(per_group):
            total = zs[group, 0, chan]
            for bit in bits:
                total = total + rs[group, bit, chan]
            out_ref[pl.ds(group * per_group + chan, rows, stride=chans), :] = total

    def spread(group):
        if group < groups:
            for bit in bits[::-1]:
                forward(group, bit).start()

    spread(0)
    spread(1)
    for copy in tables[1:]:
        copy.wait()
    pass_on(0)
    spread(2)
    if groups > 1:
        pass_on(1)
    for group in range(3, groups):
        spread(group)
    for group in range(groups):
        gather(group)
        transform(group)
        send_back(group)
        for step in range(1, n_dp):
            exchange(group, step).start()
        if group + 2 < groups:
            pass_on(group + 2)
        if group > 0:
            fold(group - 1)
    fold(groups - 1)
    for group in range(groups):
        finish(group)
        total = terms[group, dp]
        for step in range(1, n_dp):
            exchange(group, step).wait_recv()
            total = total + others[group, step]
        grad_ref[group] = total
    for group in range(groups):
        for slot in range(1, n_ctx):
            forward(group, slot).wait_send()
            inverse(group, slot).wait_send()
        for step in range(1, n_dp):
            exchange(group, step).wait_send()


def per_device(n_dp, n_ctx, output_gradient, input_spectrum, filter_spectrum):
    _, chans, tokens = output_gradient.shape
    rows = tokens // LANES
    groups = chans // 2
    per_group = chans // groups
    share = rows // n_dp
    first, last, turns, second, third = make_tables(n_ctx, tokens)

    def spectral(array):
        array = array.reshape(chans, 2, rows, LANES).transpose(0, 2, 1, 3)
        return array.reshape(chans * rows * 2, LANES)

    samples = output_gradient.reshape(chans, rows, LANES).transpose(1, 0, 2)
    samples = samples.reshape(rows * chans, LANES)
    vmem = pl.BlockSpec(memory_space=pltpu.VMEM)
    far = pl.BlockSpec(memory_space=pltpu.HBM)
    block = (groups, n_ctx, per_group, rows, LANES)
    spread = (groups, n_dp, per_group * share * 2, LANES)
    dma = pltpu.SemaphoreType.DMA
    gradient, filter_gradient = pl.pallas_call(
        functools.partial(kernel, (n_dp, n_ctx, chans, rows, groups)),
        out_shape=(
            jax.ShapeDtypeStruct((rows * chans, LANES), jnp.float32),
            jax.ShapeDtypeStruct((groups, per_group * share * 2, LANES), jnp.float32),
        ),
        in_specs=[far] * 8,
        out_specs=(vmem, vmem),
        scratch_shapes=[
            pltpu.VMEM((rows * chans, LANES), jnp.float32),
            pltpu.VMEM(first.shape[1:], jnp.bfloat16),
            pltpu.VMEM(turns.shape[1:], jnp.float32),
            pltpu.VMEM(second.shape, jnp.bfloat16),
            pltpu.VMEM((rows * chans * 2, LANES), jnp.float32),
            pltpu.VMEM((rows * chans * 2, LANES), jnp.float32),
            pltpu.VMEM(third.shape, jnp.bfloat16),
            pltpu.VMEM(last.shape[1:], jnp.bfloat16),
            pltpu.VMEM(block, jnp.float32),
            pltpu.VMEM(block, jnp.float32),
            pltpu.VMEM(block, jnp.float32),
            pltpu.VMEM(spread, jnp.float32),
            pltpu.VMEM(spread, jnp.float32),
            dma((8,)),
            dma((groups, n_ctx)),
            dma((groups, n_ctx)),
            dma((groups, n_ctx)),
            dma((groups, n_ctx)),
            dma((groups, n_dp)),
            dma((groups, n_dp)),
        ],
        compiler_params=pltpu.CompilerParams(
            collective_id=0, has_side_effects=True, vmem_limit_bytes=63 * 1024 * 1024
        ),
    )(
        samples,
        spectral(input_spectrum[0]),
        spectral(filter_spectrum),
        jnp.asarray(first),
        jnp.asarray(last),
        jnp.asarray(turns),
        jnp.asarray(second),
        jnp.asarray(third),
    )
    gradient = gradient.reshape(rows, chans, LANES).transpose(1, 0, 2)
    filter_gradient = filter_gradient.reshape(chans, share, 2, LANES).transpose(0, 2, 1, 3)
    return (
        gradient.reshape(1, chans, tokens),
        filter_gradient.reshape(chans, 2, share * LANES),
    )


def solution(mesh):
    in_specs = (P("dp", None, "ctx"), P("dp", None, None, "ctx"), P(None, None, "ctx"))
    out_specs = (P("dp", None, "ctx"), P(None, None, ("ctx", "dp")))
    return jax.shard_map(
        functools.partial(per_device, mesh.shape["dp"], mesh.shape["ctx"]),
        mesh=mesh,
        in_specs=in_specs,
        out_specs=out_specs,
        check_vma=False,
    )
```

```python
import functools
import math

import jax
import jax.numpy as jnp
import ml_dtypes
import numpy as np
from jax import lax
from jax.experimental import pallas as pl
from jax.experimental.pallas import tpu as pltpu
from jax.sharding import PartitionSpec as P

MESH = pl.DeviceIdType.MESH
LANES = 128


def reverse(index, sections):
    result = 0 * index
    for level in range(sections):
        result = result | ((index >> level) & 1) << (sections - 1 - level)
    return result


def halves(table):
    table = np.asarray(table, np.float32)
    high = table.astype(ml_dtypes.bfloat16)
    low = (table - high.astype(np.float32)).astype(ml_dtypes.bfloat16)
    return np.stack([high, low])


def make_tables(n_ctx, tokens):
    rows = tokens // LANES
    length = n_ctx * tokens
    sections = n_ctx.bit_length() - 1
    turn = 2.0 * math.pi
    ta, tb = np.arange(rows), np.arange(LANES)
    small = turn / rows * (ta[:, None] * ta[None, :] % rows)
    wide = turn / rows * (ta[:, None] * tb[None, :] % rows)
    second = np.block([[np.cos(wide), np.sin(wide)], [-np.sin(wide), np.cos(wide)]])
    third = np.block([[np.cos(small), -np.sin(small)], [np.sin(small), np.cos(small)]])
    first_all, last_all, turns_all = [], [], []
    for self_index in range(n_ctx):
        shift = reverse(self_index, sections) + 0.25
        owner = np.arange(n_ctx)
        start = (owner[:, None] * tokens + LANES * ta[None, :]).reshape(-1)
        offset = turn / length * (shift * start % length)
        angle = np.tile(small, (1, n_ctx)) + offset[None, :]
        first_all.append(halves(np.concatenate([np.cos(angle), -np.sin(angle)], axis=0)))
        angle = np.tile(wide, (n_ctx, 1)) + offset[:, None]
        last_all.append(
            halves(np.concatenate([np.cos(angle), -np.sin(angle)], axis=1) / length)
        )
        angle = turn / length * (tb[None, :] * (n_ctx * tb[:, None] + shift) % length)
        turns_all.append(
            np.stack([np.cos(angle), -np.sin(angle), np.cos(angle).T, np.sin(angle).T])
        )
    return (
        np.stack(first_all),
        np.stack(last_all),
        np.stack(turns_all).astype(np.float32),
        halves(second),
        halves(third),
    )


def split(value):
    high = value.astype(jnp.bfloat16)
    return high, (value - high.astype(jnp.float32)).astype(jnp.bfloat16)


def product(table, value, contract):
    high, low = split(value)
    dims = (((1,), (contract,)), ((), ()))
    dot = functools.partial(
        lax.dot_general, dimension_numbers=dims, preferred_element_type=jnp.float32
    )
    return dot(table[0], high) + (dot(table[0], low) + dot(table[1], high))


def kernel(
    sizes,
    x_hbm,
    saved_hbm,
    filt_hbm,
    first_hbm,
    last_hbm,
    turns_hbm,
    second_hbm,
    third_hbm,
    out_ref,
    grad_ref,
    x_ref,
    first_ref,
    turns_ref,
    second_ref,
    saved_ref,
    filt_ref,
    third_ref,
    last_ref,
    xs,
    zs,
    rs,
    terms,
    others,
    table_sem,
    fwd_send,
    fwd_recv,
    inv_send,
    inv_recv,
    dp_send,
    dp_recv,
):
    n_dp, n_ctx, chans, rows, groups = sizes
    per_group = chans // groups
    share = rows // n_dp
    repeats = LANES // rows
    dp = lax.axis_index("dp")
    ctx = lax.axis_index("ctx")
    peers = [lax.rem(dp + step, n_dp) for step in range(n_dp)]

    tables = [
        pltpu.make_async_copy(source, target, table_sem.at[number])
        for number, (source, target) in enumerate(
            [
                (x_hbm, x_ref),
                (first_hbm.at[ctx], first_ref),
                (turns_hbm.at[ctx], turns_ref),
                (second_hbm, second_ref),
                (saved_hbm, saved_ref),
                (filt_hbm, filt_ref),
                (third_hbm, third_ref),
                (last_hbm.at[ctx], last_ref),
            ]
        )
    ]
    for copy in tables:
        copy.start()

    barrier = pltpu.get_barrier_semaphore()
    for way in (1, n_ctx - 1):
        near = (dp, lax.rem(ctx + way, n_ctx))
        pl.semaphore_signal(barrier, inc=1, device_id=near, device_id_type=MESH)
    for peer in peers[1:]:
        pl.semaphore_signal(barrier, inc=1, device_id=(peer, ctx), device_id_type=MESH)

    tables[0].wait()
    for chan in range(chans):
        xs[chan // per_group, ctx, chan % per_group] = x_ref[pl.ds(chan, rows, stride=chans), :]
    pl.semaphore_wait(barrier, 2 + n_dp - 1)

    def forward(group, slot, way):
        return pltpu.make_async_remote_copy(
            src_ref=xs.at[group, slot],
            dst_ref=xs.at[group, slot],
            send_sem=fwd_send.at[(way + 1) // 2, group, slot],
            recv_sem=fwd_recv.at[group, slot],
            device_id=(dp, lax.rem(ctx + way + n_ctx, n_ctx)),
            device_id_type=MESH,
        )

    def inverse(group, slot, way):
        return pltpu.make_async_remote_copy(
            src_ref=zs.at[group, slot],
            dst_ref=rs.at[(way + 1) // 2, group, slot],
            send_sem=inv_send.at[group, slot],
            recv_sem=inv_recv.at[(way + 1) // 2, group, slot],
            device_id=(dp, lax.rem(ctx + way + n_ctx, n_ctx)),
            device_id_type=MESH,
        )

    def has(way, steps):
        return ctx + steps < n_ctx if way > 0 else ctx >= steps

    def exchange(group, step):
        return pltpu.make_async_remote_copy(
            src_ref=terms.at[group, peers[step]],
            dst_ref=others.at[group, step],
            send_sem=dp_send.at[group, step],
            recv_sem=dp_recv.at[group, step],
            device_id=(peers[step], ctx),
            device_id_type=MESH,
        )

    def arrive(group, step, on):
        for way in (1, -1):

            @pl.when(has(-way, step))
            def _():
                forward(group, ctx - way * step, way).wait_recv()

            if on:

                @pl.when(has(-way, step) & has(way, 1))
                def _():
                    forward(group, ctx - way * step, way).start()

    def pass_on(group):
        for step in range(1, n_ctx - 1):
            arrive(group, step, True)

    def gather(group):
        arrive(group, n_ctx - 1, False)

    def transform(group):
        pair = range(per_group)
        block = jnp.concatenate(
            [xs[group, :, chan].reshape(n_ctx * rows, LANES) for chan in pair], axis=1
        )
        stage = product(first_ref, block, 0)
        turned = []
        for chan in pair:
            lanes = slice(chan * LANES, (chan + 1) * LANES)
            real = jnp.concatenate([stage[:rows, lanes]] * repeats, axis=0)
            imag = jnp.concatenate([stage[rows:, lanes]] * repeats, axis=0)
            cosine, sine = turns_ref[0], turns_ref[1]
            turned.append(
                jnp.concatenate(
                    [real * cosine - imag * sine, real * sine + imag * cosine], axis=1
                )
            )
        spectrum = product(second_ref, jnp.concatenate(turned, axis=0), 1)
        multiplied = []
        for chan in pair:
            lanes = slice(chan * LANES, (chan + 1) * LANES)
            real, imag = spectrum[:rows, lanes], spectrum[rows:, lanes]
            base = (group * per_group + chan) * 2 * rows
            saved_real = saved_ref[pl.ds(base, rows, stride=2), :]
            saved_imag = saved_ref[pl.ds(base + 1, rows, stride=2), :]
            parts = (real * saved_real + imag * saved_imag, imag * saved_real - real * saved_imag)
            for number, part in enumerate(parts):
                for owner in range(n_dp):
                    where = pl.ds(chan * 2 * share + number, share, stride=2)
                    terms[group, owner, where, :] = part[owner * share : (owner + 1) * share]
            filt_real = filt_ref[pl.ds(base, rows, stride=2), :]
            filt_imag = filt_ref[pl.ds(base + 1, rows, stride=2), :]
            multiplied.append(
                jnp.concatenate(
                    [real * filt_real + imag * filt_imag, imag * filt_real - real * filt_imag],
                    axis=0,
                )
            )
        stage = product(third_ref, jnp.concatenate(multiplied, axis=1), 0)
        turned = []
        for chan in pair:
            lanes = slice(chan * LANES, (chan + 1) * LANES)
            real = jnp.concatenate([stage[:rows, lanes]] * repeats, axis=0)
            imag = jnp.concatenate([stage[rows:, lanes]] * repeats, axis=0)
            cosine, sine = turns_ref[2], turns_ref[3]
            turned.append(
                jnp.concatenate(
                    [real * cosine - imag * sine, real * sine + imag * cosine], axis=1
                )
            )
        result = product(last_ref, jnp.concatenate(turned, axis=0), 1)
        for chan in pair:
            lanes = slice(chan * LANES, (chan + 1) * LANES)
            zs[group, :, chan] = result[:, lanes].reshape(n_ctx, rows, LANES)

    def send_back(group):
        for step in range(n_ctx - 1, 0, -1):
            for way in (1, -1):

                @pl.when(has(way, step) & jnp.logical_not(has(-way, 1)))
                def _():
                    inverse(group, ctx + way * step, way).start()

    def fold(group):
        for step in range(n_ctx - 1, 0, -1):
            for way in (1, -1):
                slot = ctx + way * step

                @pl.when(has(way, step) & has(-way, 1))
                def _():
                    inverse(group, slot, way).wait_recv()
                    zs[group, slot] = zs[group, slot] + rs[(way + 1) // 2, group, slot]
                    inverse(group, slot, way).start()

    def finish(group):
        for way in (1, -1):

            @pl.when(has(-way, 1))
            def _():
                inverse(group, ctx, way).wait_recv()
                zs[group, ctx] = zs[group, ctx] + rs[(way + 1) // 2, group, ctx]

        for chan in range(per_group):
            where = pl.ds(group * per_group + chan, rows, stride=chans)
            out_ref[where, :] = zs[group, ctx, chan]

    def spread(group):
        if group < groups:
            for way in (1, -1):

                @pl.when(has(way, 1))
                def _():
                    forward(group, ctx, way).start()

    spread(0)
    spread(1)
    for copy in tables[1:]:
        copy.wait()
    pass_on(0)
    spread(2)
    if groups > 1:
        pass_on(1)
    for group in range(3, groups):
        spread(group)
    for group in range(groups):
        gather(group)
        transform(group)
        send_back(group)
        for step in range(1, n_dp):
            exchange(group, step).start()
        if group + 2 < groups:
            pass_on(group + 2)
        if group > 0:
            fold(group - 1)
    fold(groups - 1)
    for group in range(groups):
        finish(group)
        total = terms[group, dp]
        for step in range(1, n_dp):
            exchange(group, step).wait_recv()
            total = total + others[group, step]
        grad_ref[group] = total
    for group in range(groups):
        for way in (1, -1):
            for step in range(n_ctx - 1):

                @pl.when(has(-way, step) & has(way, 1))
                def _():
                    forward(group, ctx - way * step, way).wait_send()

            for step in range(1, n_ctx):

                @pl.when(has(way, step))
                def _():
                    inverse(group, ctx + way * step, way).wait_send()

        for step in range(1, n_dp):
            exchange(group, step).wait_send()


def per_device(n_dp, n_ctx, output_gradient, input_spectrum, filter_spectrum):
    _, chans, tokens = output_gradient.shape
    rows = tokens // LANES
    groups = chans // 2
    per_group = chans // groups
    share = rows // n_dp
    first, last, turns, second, third = make_tables(n_ctx, tokens)

    def spectral(array):
        array = array.reshape(chans, 2, rows, LANES).transpose(0, 2, 1, 3)
        return array.reshape(chans * rows * 2, LANES)

    samples = output_gradient.reshape(chans, rows, LANES).transpose(1, 0, 2)
    samples = samples.reshape(rows * chans, LANES)
    vmem = pl.BlockSpec(memory_space=pltpu.VMEM)
    far = pl.BlockSpec(memory_space=pltpu.HBM)
    block = (groups, n_ctx, per_group, rows, LANES)
    spread = (groups, n_dp, per_group * share * 2, LANES)
    dma = pltpu.SemaphoreType.DMA
    gradient, filter_gradient = pl.pallas_call(
        functools.partial(kernel, (n_dp, n_ctx, chans, rows, groups)),
        out_shape=(
            jax.ShapeDtypeStruct((rows * chans, LANES), jnp.float32),
            jax.ShapeDtypeStruct((groups, per_group * share * 2, LANES), jnp.float32),
        ),
        in_specs=[far] * 8,
        out_specs=(vmem, vmem),
        scratch_shapes=[
            pltpu.VMEM((rows * chans, LANES), jnp.float32),
            pltpu.VMEM(first.shape[1:], jnp.bfloat16),
            pltpu.VMEM(turns.shape[1:], jnp.float32),
            pltpu.VMEM(second.shape, jnp.bfloat16),
            pltpu.VMEM((rows * chans * 2, LANES), jnp.float32),
            pltpu.VMEM((rows * chans * 2, LANES), jnp.float32),
            pltpu.VMEM(third.shape, jnp.bfloat16),
            pltpu.VMEM(last.shape[1:], jnp.bfloat16),
            pltpu.VMEM(block, jnp.float32),
            pltpu.VMEM(block, jnp.float32),
            pltpu.VMEM((2,) + block, jnp.float32),
            pltpu.VMEM(spread, jnp.float32),
            pltpu.VMEM(spread, jnp.float32),
            dma((8,)),
            dma((2, groups, n_ctx)),
            dma((groups, n_ctx)),
            dma((groups, n_ctx)),
            dma((2, groups, n_ctx)),
            dma((groups, n_dp)),
            dma((groups, n_dp)),
        ],
        compiler_params=pltpu.CompilerParams(
            collective_id=0, has_side_effects=True, vmem_limit_bytes=63 * 1024 * 1024
        ),
    )(
        samples,
        spectral(input_spectrum[0]),
        spectral(filter_spectrum),
        jnp.asarray(first),
        jnp.asarray(last),
        jnp.asarray(turns),
        jnp.asarray(second),
        jnp.asarray(third),
    )
    gradient = gradient.reshape(rows, chans, LANES).transpose(1, 0, 2)
    filter_gradient = filter_gradient.reshape(chans, share, 2, LANES).transpose(0, 2, 1, 3)
    return (
        gradient.reshape(1, chans, tokens),
        filter_gradient.reshape(chans, 2, share * LANES),
    )


def solution(mesh):
    in_specs = (P("dp", None, "ctx"), P("dp", None, None, "ctx"), P(None, None, "ctx"))
    out_specs = (P("dp", None, "ctx"), P(None, None, ("ctx", "dp")))
    return jax.shard_map(
        functools.partial(per_device, mesh.shape["dp"], mesh.shape["ctx"]),
        mesh=mesh,
        in_specs=in_specs,
        out_specs=out_specs,
        check_vma=False,
    )
```

```python
import functools
import math

import jax
import jax.numpy as jnp
import ml_dtypes
import numpy as np
from jax import lax
from jax.experimental import pallas as pl
from jax.experimental.pallas import tpu as pltpu
from jax.sharding import PartitionSpec as P

MESH = pl.DeviceIdType.MESH
LANES = 128


def low_bit(value):
    return value & -value


def reverse(index, sections):
    result = 0 * index
    for level in range(sections):
        result = result | ((index >> level) & 1) << (sections - 1 - level)
    return result


def halves(table):
    table = np.asarray(table, np.float32)
    high = table.astype(ml_dtypes.bfloat16)
    low = (table - high.astype(np.float32)).astype(ml_dtypes.bfloat16)
    return np.stack([high, low])


def make_tables(n_ctx, tokens):
    rows = tokens // LANES
    length = n_ctx * tokens
    sections = n_ctx.bit_length() - 1
    turn = 2.0 * math.pi
    ta, tb = np.arange(rows), np.arange(LANES)
    small = turn / rows * (ta[:, None] * ta[None, :] % rows)
    wide = turn / rows * (ta[:, None] * tb[None, :] % rows)
    second = np.block([[np.cos(wide), np.sin(wide)], [-np.sin(wide), np.cos(wide)]])
    third = np.block([[np.cos(small), -np.sin(small)], [np.sin(small), np.cos(small)]])
    first_all, last_all, turns_all = [], [], []
    for self_index in range(n_ctx):
        shift = reverse(self_index, sections) + 0.25
        owner = self_index ^ np.arange(n_ctx)
        start = (owner[:, None] * tokens + LANES * ta[None, :]).reshape(-1)
        offset = turn / length * (shift * start % length)
        angle = np.tile(small, (1, n_ctx)) + offset[None, :]
        first_all.append(halves(np.concatenate([np.cos(angle), -np.sin(angle)], axis=0)))
        angle = np.tile(wide, (n_ctx, 1)) + offset[:, None]
        last_all.append(
            halves(np.concatenate([np.cos(angle), -np.sin(angle)], axis=1) / length)
        )
        angle = turn / length * (tb[None, :] * (n_ctx * tb[:, None] + shift) % length)
        turns_all.append(
            np.stack([np.cos(angle), -np.sin(angle), np.cos(angle).T, np.sin(angle).T])
        )
    return (
        np.stack(first_all),
        np.stack(last_all),
        np.stack(turns_all).astype(np.float32),
        halves(second),
        halves(third),
    )


def split(value):
    high = value.astype(jnp.bfloat16)
    return high, (value - high.astype(jnp.float32)).astype(jnp.bfloat16)


def product(table, value, contract):
    high, low = split(value)
    dims = (((1,), (contract,)), ((), ()))
    dot = functools.partial(
        lax.dot_general, dimension_numbers=dims, preferred_element_type=jnp.float32
    )
    return dot(table[0], high) + (dot(table[0], low) + dot(table[1], high))


def kernel(
    sizes,
    x_hbm,
    saved_hbm,
    filt_hbm,
    first_hbm,
    last_hbm,
    turns_hbm,
    second_hbm,
    third_hbm,
    out_ref,
    grad_ref,
    x_ref,
    first_ref,
    turns_ref,
    second_ref,
    saved_ref,
    filt_ref,
    third_ref,
    last_ref,
    xs,
    zs,
    rs,
    terms,
    others,
    table_sem,
    fwd_send,
    fwd_recv,
    inv_send,
    inv_recv,
    dp_send,
    dp_recv,
):
    n_dp, n_ctx, chans, rows, groups = sizes
    per_group = chans // groups
    share = rows // n_dp
    repeats = LANES // rows
    dp = lax.axis_index("dp")
    ctx = lax.axis_index("ctx")
    bits = [1 << level for level in range(n_ctx.bit_length() - 1)]
    peers = [lax.rem(dp + step, n_dp) for step in range(n_dp)]

    tables = [
        pltpu.make_async_copy(source, target, table_sem.at[number])
        for number, (source, target) in enumerate(
            [
                (x_hbm, x_ref),
                (first_hbm.at[ctx], first_ref),
                (turns_hbm.at[ctx], turns_ref),
                (second_hbm, second_ref),
                (saved_hbm, saved_ref),
                (filt_hbm, filt_ref),
                (third_hbm, third_ref),
                (last_hbm.at[ctx], last_ref),
            ]
        )
    ]
    for copy in tables:
        copy.start()

    barrier = pltpu.get_barrier_semaphore()
    for bit in bits:
        pl.semaphore_signal(barrier, inc=1, device_id=(dp, ctx ^ bit), device_id_type=MESH)
    for peer in peers[1:]:
        pl.semaphore_signal(barrier, inc=1, device_id=(peer, ctx), device_id_type=MESH)

    tables[0].wait()
    for chan in range(chans):
        xs[chan // per_group, 0, chan % per_group] = x_ref[pl.ds(chan, rows, stride=chans), :]
    pl.semaphore_wait(barrier, len(bits) + n_dp - 1)

    def forward(group, slot):
        bit = low_bit(slot)
        return pltpu.make_async_remote_copy(
            src_ref=xs.at[group, slot - bit],
            dst_ref=xs.at[group, slot],
            send_sem=fwd_send.at[group, slot],
            recv_sem=fwd_recv.at[group, slot],
            device_id=(dp, ctx ^ bit),
            device_id_type=MESH,
        )

    def inverse(group, slot):
        return pltpu.make_async_remote_copy(
            src_ref=zs.at[group, slot],
            dst_ref=rs.at[group, slot],
            send_sem=inv_send.at[group, slot],
            recv_sem=inv_recv.at[group, slot],
            device_id=(dp, ctx ^ low_bit(slot)),
            device_id_type=MESH,
        )

    def exchange(group, step):
        return pltpu.make_async_remote_copy(
            src_ref=terms.at[group, peers[step]],
            dst_ref=others.at[group, step],
            send_sem=dp_send.at[group, step],
            recv_sem=dp_recv.at[group, step],
            device_id=(peers[step], ctx),
            device_id_type=MESH,
        )

    def pass_on(group):
        for bit in bits[::-1]:
            for slot in range(2 * bit, n_ctx, 2 * bit):
                if low_bit(slot) == 2 * bit:
                    forward(group, slot).wait_recv()
                forward(group, slot + bit).start()

    def gather(group):
        for slot in range(1, n_ctx, 2):
            forward(group, slot).wait_recv()

    def transform(group):
        pair = range(per_group)
        block = jnp.concatenate(
            [xs[group, :, chan].reshape(n_ctx * rows, LANES) for chan in pair], axis=1
        )
        stage = product(first_ref, block, 0)
        turned = []
        for chan in pair:
            lanes = slice(chan * LANES, (chan + 1) * LANES)
            real = jnp.concatenate([stage[:rows, lanes]] * repeats, axis=0)
            imag = jnp.concatenate([stage[rows:, lanes]] * repeats, axis=0)
            cosine, sine = turns_ref[0], turns_ref[1]
            turned.append(
                jnp.concatenate(
                    [real * cosine - imag * sine, real * sine + imag * cosine], axis=1
                )
            )
        spectrum = product(second_ref, jnp.concatenate(turned, axis=0), 1)
        multiplied = []
        for chan in pair:
            lanes = slice(chan * LANES, (chan + 1) * LANES)
            real, imag = spectrum[:rows, lanes], spectrum[rows:, lanes]
            base = (group * per_group + chan) * 2 * rows
            saved_real = saved_ref[pl.ds(base, rows, stride=2), :]
            saved_imag = saved_ref[pl.ds(base + 1, rows, stride=2), :]
            parts = (real * saved_real + imag * saved_imag, imag * saved_real - real * saved_imag)
            for number, part in enumerate(parts):
                for owner in range(n_dp):
                    where = pl.ds(chan * 2 * share + number, share, stride=2)
                    terms[group, owner, where, :] = part[owner * share : (owner + 1) * share]
            filt_real = filt_ref[pl.ds(base, rows, stride=2), :]
            filt_imag = filt_ref[pl.ds(base + 1, rows, stride=2), :]
            multiplied.append(
                jnp.concatenate(
                    [real * filt_real + imag * filt_imag, imag * filt_real - real * filt_imag],
                    axis=0,
                )
            )
        stage = product(third_ref, jnp.concatenate(multiplied, axis=1), 0)
        turned = []
        for chan in pair:
            lanes = slice(chan * LANES, (chan + 1) * LANES)
            real = jnp.concatenate([stage[:rows, lanes]] * repeats, axis=0)
            imag = jnp.concatenate([stage[rows:, lanes]] * repeats, axis=0)
            cosine, sine = turns_ref[2], turns_ref[3]
            turned.append(
                jnp.concatenate(
                    [real * cosine - imag * sine, real * sine + imag * cosine], axis=1
                )
            )
        result = product(last_ref, jnp.concatenate(turned, axis=0), 1)
        for chan in pair:
            lanes = slice(chan * LANES, (chan + 1) * LANES)
            zs[group, :, chan] = result[:, lanes].reshape(n_ctx, rows, LANES)

    def send_back(group):
        for slot in range(1, n_ctx, 2):
            inverse(group, slot).start()

    def fold(group):
        for bit in bits[:-1]:
            for slot in range(2 * bit, n_ctx, 2 * bit):
                inverse(group, slot + bit).wait_recv()
                zs[group, slot] = zs[group, slot] + rs[group, slot + bit]
                if low_bit(slot) == 2 * bit:
                    inverse(group, slot).start()

    def finish(group):
        for bit in bits:
            inverse(group, bit).wait_recv()
        for chan in range(per_group):
            total = zs[group, 0, chan]
            for bit in bits:
                total = total + rs[group, bit, chan]
            out_ref[pl.ds(group * per_group + chan, rows, stride=chans), :] = total

    def spread(group):
        if group < groups:
            for bit in bits[::-1]:
                forward(group, bit).start()

    spread(0)
    spread(1)
    for copy in tables[1:]:
        copy.wait()
    pass_on(0)
    spread(2)
    if groups > 1:
        pass_on(1)
    for group in range(3, groups):
        spread(group)
    for group in range(groups):
        gather(group)
        transform(group)
        send_back(group)
        for step in range(1, n_dp):
            exchange(group, step).start()
        if group + 2 < groups:
            pass_on(group + 2)
        if group > 0:
            fold(group - 1)
    fold(groups - 1)
    for group in range(groups):
        finish(group)
        total = terms[group, dp]
        for step in range(1, n_dp):
            exchange(group, step).wait_recv()
            total = total + others[group, step]
        grad_ref[group] = total
    for group in range(groups):
        for slot in range(1, n_ctx):
            forward(group, slot).wait_send()
            inverse(group, slot).wait_send()
        for step in range(1, n_dp):
            exchange(group, step).wait_send()


def per_device(n_dp, n_ctx, output_gradient, input_spectrum, filter_spectrum):
    _, chans, tokens = output_gradient.shape
    rows = tokens // LANES
    groups = chans // 4
    per_group = chans // groups
    share = rows // n_dp
    first, last, turns, second, third = make_tables(n_ctx, tokens)

    def spectral(array):
        array = array.reshape(chans, 2, rows, LANES).transpose(0, 2, 1, 3)
        return array.reshape(chans * rows * 2, LANES)

    samples = output_gradient.reshape(chans, rows, LANES).transpose(1, 0, 2)
    samples = samples.reshape(rows * chans, LANES)
    vmem = pl.BlockSpec(memory_space=pltpu.VMEM)
    far = pl.BlockSpec(memory_space=pltpu.HBM)
    block = (groups, n_ctx, per_group, rows, LANES)
    spread = (groups, n_dp, per_group * share * 2, LANES)
    dma = pltpu.SemaphoreType.DMA
    gradient, filter_gradient = pl.pallas_call(
        functools.partial(kernel, (n_dp, n_ctx, chans, rows, groups)),
        out_shape=(
            jax.ShapeDtypeStruct((rows * chans, LANES), jnp.float32),
            jax.ShapeDtypeStruct((groups, per_group * share * 2, LANES), jnp.float32),
        ),
        in_specs=[far] * 8,
        out_specs=(vmem, vmem),
        scratch_shapes=[
            pltpu.VMEM((rows * chans, LANES), jnp.float32),
            pltpu.VMEM(first.shape[1:], jnp.bfloat16),
            pltpu.VMEM(turns.shape[1:], jnp.float32),
            pltpu.VMEM(second.shape, jnp.bfloat16),
            pltpu.VMEM((rows * chans * 2, LANES), jnp.float32),
            pltpu.VMEM((rows * chans * 2, LANES), jnp.float32),
            pltpu.VMEM(third.shape, jnp.bfloat16),
            pltpu.VMEM(last.shape[1:], jnp.bfloat16),
            pltpu.VMEM(block, jnp.float32),
            pltpu.VMEM(block, jnp.float32),
            pltpu.VMEM(block, jnp.float32),
            pltpu.VMEM(spread, jnp.float32),
            pltpu.VMEM(spread, jnp.float32),
            dma((8,)),
            dma((groups, n_ctx)),
            dma((groups, n_ctx)),
            dma((groups, n_ctx)),
            dma((groups, n_ctx)),
            dma((groups, n_dp)),
            dma((groups, n_dp)),
        ],
        compiler_params=pltpu.CompilerParams(
            collective_id=0, has_side_effects=True, vmem_limit_bytes=56 * 1024 * 1024
        ),
    )(
        samples,
        spectral(input_spectrum[0]),
        spectral(filter_spectrum),
        jnp.asarray(first),
        jnp.asarray(last),
        jnp.asarray(turns),
        jnp.asarray(second),
        jnp.asarray(third),
    )
    gradient = gradient.reshape(rows, chans, LANES).transpose(1, 0, 2)
    filter_gradient = filter_gradient.reshape(chans, share, 2, LANES).transpose(0, 2, 1, 3)
    return (
        gradient.reshape(1, chans, tokens),
        filter_gradient.reshape(chans, 2, share * LANES),
    )


def solution(mesh):
    in_specs = (P("dp", None, "ctx"), P("dp", None, None, "ctx"), P(None, None, "ctx"))
    out_specs = (P("dp", None, "ctx"), P(None, None, ("ctx", "dp")))
    return jax.shard_map(
        functools.partial(per_device, mesh.shape["dp"], mesh.shape["ctx"]),
        mesh=mesh,
        in_specs=in_specs,
        out_specs=out_specs,
        check_vma=False,
    )
```
